256 devices in a mesh: dp: 64 (over z_hi, y, x), tensor: 4 (over z_lo, core).
Axes of the slice: x: 4, y: 4, z: 8 (z_hi: 4, z_lo: 2; z = z_hi * 2 + z_lo), core: 2. Of those that a mesh axis runs over, the one named last changes fastest.
Arguments:
- acts: bfloat16 [65536, 8192], P(('dp', 'tensor')), may hold values from -24 to 24
- grad_out: bfloat16 [65536, 1024], P(('dp', 'tensor')), may hold values from -0.0234375 to 0.0234375
- master: float32 [8192, 1024], P('dp', 'tensor'), may hold values from -0.125 to 0.125
- moment1: float32 [8192, 1024], P('dp', 'tensor'), may hold values from -1.75 to 1.75
- moment2: float32 [8192, 1024], P('dp', 'tensor'), may hold values from 0.0001 to 0.002
Outputs:
- new_master: float32 [8192, 1024], P('dp', 'tensor')
- new_moment1: float32 [8192, 1024], P('dp', 'tensor')
- new_moment2: float32 [8192, 1024], P('dp', 'tensor')
- new_weights: bfloat16 [8192, 1024], P(None, 'tensor')
The draws below stay inside these ranges and needn't reach their ends.
All inputs are finite; a program needn't handle non-finite values.
Results may differ from the reference program's by a relative error of at most 0.001.
Values may be sent and summed in bfloat16 or wider, within the bound.
No kernel may reach another device: no remote copies, remote signals or barrier semaphores. Data moves between devices by JAX's collectives and lax.ppermute only.
A program may use at most 128 MiB of HBM per device.

```python
import math
import jax
import jax.numpy as jnp
from jax import lax

D = 8192
KV = 1024
TOKENS = 65536
N_DP = 64


def spiked(entries, own_key, source, target, blocks, factor):
    owner, partner = [(jnp.arange(entries.shape[dim]) // (entries.shape[dim] // blocks)).reshape([-1 if axis == dim else 1 for axis in range(entries.ndim)]) for dim in (source, target)]
    chosen = jax.random.permutation(own_key, blocks)[partner]
    strong = (owner == chosen) | (owner == (partner + blocks // 2) % blocks)
    return jnp.where(strong, factor * entries, entries)


def levels(rng, shape, cuts, smallest, largest):
    level = 1.0
    for position, shards_of in cuts:
        steps = jax.random.uniform(jax.random.fold_in(jax.random.fold_in(rng, 6), position), (shards_of,), jnp.float32, smallest / len(cuts), largest / len(cuts))
        level = level * jnp.repeat(jnp.exp(steps), shape[position] // shards_of).reshape((-1,) + (1,) * (len(shape) - 1 - position))
    return level


def scatter_about(own_key, dims, spread, limit, shards=(), kind=jnp.bfloat16):
    array = spread * jax.random.normal(own_key, dims, jnp.float32)
    if shards:
        array = array * levels(own_key, dims, shards, -0.22, 0.18)
    return jnp.clip(array, -limit, limit).astype(kind)


def gaussian_with(stream_key, shape, spread, most, cuts, heavy, kind=jnp.bfloat16):
    entries = spread * jax.random.normal(stream_key, shape, jnp.float32)
    if cuts:
        entries = entries * levels(stream_key, shape, cuts, -0.22, 0.18)
    return jnp.clip(spiked(entries, jax.random.fold_in(stream_key, 3), *heavy), -most, most).astype(kind)


def setup_inputs(seed: int = 0) -> dict:
    streams_of = jax.random.split(jax.random.key(seed), 6)
    acts = gaussian_with(streams_of[0], (TOKENS, D), 1.0, 24.0, ((0, 256),), (0, 1, 256, 6.0))
    grad_out = scatter_about(streams_of[1], (TOKENS, KV), (TOKENS ** -0.5), 0.0234375, ((0, 256),))
    master = scatter_about(streams_of[2], (D, KV), 0.02, 0.125, ((0, 64), (1, 4)), jnp.float32)
    moment1 = scatter_about(streams_of[3], (D, KV), 0.3, 1.75, ((0, 64), (1, 4)), jnp.float32)
    moment2 = jnp.clip(jnp.exp(math.log(0.002) - 2.9957323 * jax.random.uniform(streams_of[4], (D, KV), jnp.float32) ** levels(streams_of[4], (D, KV), ((0, 64), (1, 4)), -0.2, 0.2)), 0.0001, 0.002)
    return {"acts": acts, "grad_out": grad_out, "master": master, "moment1": moment1, "moment2": moment2}


first_bias = 1.0 - math.exp(100.0 * math.log(0.9))
second_bias = 1.0 - math.exp(100.0 * math.log(0.999))

def reference(acts, grad_out, master, moment1, moment2):
    groups = N_DP
    rows = acts.shape[0] // groups
    acts_blocks = acts.reshape(groups, rows, acts.shape[1])
    grad_blocks = grad_out.reshape(groups, rows, grad_out.shape[1])

    def accumulate(total, pair):
        block_acts, block_grad = pair
        return (total + lax.dot_general(block_acts.astype(jnp.float32), block_grad.astype(jnp.float32), (((0,), (0,)), ((), ())), precision=lax.Precision.HIGHEST, preferred_element_type=jnp.float32), None)
    start = jnp.zeros((acts.shape[1], grad_out.shape[1]), jnp.float32)
    grad, unused = lax.scan(accumulate, start, (acts_blocks, grad_blocks))
    new_moment1 = 0.9 * moment1 + 0.1 * grad
    new_moment2 = 0.999 * moment2 + 0.001 * grad * grad
    update = new_moment1 / first_bias / (jnp.sqrt(new_moment2 / second_bias) + 1e-08)
    new_master = master - 0.01 * (update + 0.1 * master)
    return (new_master, new_moment1, new_moment2, new_master.astype(jnp.bfloat16))
```

```python
import math

import jax
import jax.numpy as jnp
from jax import lax
from jax.experimental import pallas as pl
from jax.experimental.pallas import tpu as pltpu
from jax.sharding import Mesh
from jax.sharding import PartitionSpec as P

first_bias = 1.0 - math.exp(100.0 * math.log(0.9))
second_bias = 1.0 - math.exp(100.0 * math.log(0.999))

F32, F16, BF16 = jnp.float32, jnp.float16, jnp.bfloat16
LANES = 128


def shift(array, axis, by, size=4):
    return lax.ppermute(array, axis, [(i, (i + by) % size) for i in range(size)])


def other_core(array):
    return lax.ppermute(array, "c", [(0, 1), (1, 0)])


def arrange(acts, where):
    tokens = acts.shape[0]

    def kernel(where_ref, acts_ref, out_ref, sem):
        x, y = where_ref[0], where_ref[1]
        copies = []
        for colour in range(2):
            for first in range(4):
                for second in range(4):
                    kx, ky = (first, second) if colour == 0 else (second, first)
                    for half in range(2):
                        block = (
                            (2 * colour + half) * 16
                            + lax.rem(y + ky, 4) * 4
                            + lax.rem(x + kx, 4)
                        )
                        copies.append(
                            pltpu.make_async_copy(
                                acts_ref.at[
                                    :, pl.ds(pl.multiple_of(block * LANES, LANES), LANES)
                                ],
                                out_ref.at[
                                    colour * 4 + first,
                                    :,
                                    pl.ds((second * 2 + half) * LANES, LANES),
                                ],
                                sem,
                            )
                        )
        for copy in copies:
            copy.start()
        for copy in copies:
            copy.wait()

    return pl.pallas_call(
        kernel,
        out_shape=jax.ShapeDtypeStruct((8, tokens, 1024), acts.dtype),
        in_specs=[
            pl.BlockSpec(memory_space=pltpu.SMEM),
            pl.BlockSpec(memory_space=pl.ANY),
        ],
        out_specs=pl.BlockSpec(memory_space=pl.ANY),
        scratch_shapes=[pltpu.SemaphoreType.DMA],
        cost_estimate=pl.CostEstimate(
            flops=0, bytes_accessed=4 * acts.size, transcendentals=0
        ),
    )(where, acts)


def assemble(pieces, where):
    def kernel(where_ref, *refs):
        ins, out_ref, sem = refs[:8], refs[8], refs[9]
        x, y, zh = where_ref[0], where_ref[1], where_ref[2]
        copies = []
        for colour in range(2):
            for first in range(4):
                for second in range(4):
                    kx, ky = (second, first) if colour == 0 else (first, second)
                    for half in range(2):
                        kz = 2 * colour + half
                        block = (
                            lax.rem(zh + 4 - kz, 4) * 16
                            + lax.rem(y + 4 - ky, 4) * 4
                            + lax.rem(x + 4 - kx, 4)
                        )
                        copies.append(
                            pltpu.make_async_copy(
                                ins[colour * 4 + first].at[
                                    pl.ds((second * 2 + half) * LANES, LANES), :
                                ],
                                out_ref.at[
                                    pl.ds(pl.multiple_of(block * LANES, LANES), LANES), :
                                ],
                                sem,
                            )
                        )
        for copy in copies:
            copy.start()
        for copy in copies:
            copy.wait()

    return pl.pallas_call(
        kernel,
        out_shape=jax.ShapeDtypeStruct((8192, 256), BF16),
        in_specs=[pl.BlockSpec(memory_space=pltpu.SMEM)]
        + [pl.BlockSpec(memory_space=pl.ANY)] * 8,
        out_specs=pl.BlockSpec(memory_space=pl.ANY),
        scratch_shapes=[pltpu.SemaphoreType.DMA],
    )(where, *pieces[0], *pieces[1])


def dot(a, b):
    return lax.dot_general(a, b, (((0,), (0,)), ((), ())), preferred_element_type=F32)


def per_device(acts, grad_out, master, moment1, moment2):
    x, y, zh, core = (lax.axis_index(name) for name in ("x", "y", "zh", "c"))
    where = jnp.stack([x, y, zh]).astype(jnp.int32)

    parts = grad_out.reshape(-1, 2, 2, 256)
    mine = jnp.where(core == 0, parts[:, :, 0], parts[:, :, 1]).reshape(-1, 512)
    theirs = jnp.where(core == 0, parts[:, :, 1], parts[:, :, 0]).reshape(-1, 512)
    peer_grad = other_core(theirs)
    chunks = arrange(acts, where)
    order = (2, 6, 1, 5, 3, 7, 0, 4)
    partial = {}
    for i in order:
        peer = other_core(chunks[i])
        partial[i] = dot(chunks[i], mine) + dot(peer, peer_grad)

    def reduce(parts_by_distance, axis, scale):
        total = parts_by_distance[0]
        for by in (2, 1, 3):
            sent = (parts_by_distance[by] * scale).astype(F16)
            total = total + shift(sent, axis, by).astype(F32) * (1.0 / scale)
        return total

    sum_x = reduce([partial[k] for k in range(4)], "x", 128.0)
    sum_y = reduce([partial[4 + k] for k in range(4)], "y", 128.0)
    sum_xy = reduce([sum_x[k * 256 : (k + 1) * 256] for k in range(4)], "y", 32.0)
    sum_yx = reduce([sum_y[k * 256 : (k + 1) * 256] for k in range(4)], "x", 32.0)
    level = jnp.concatenate([sum_xy, sum_yx], 0)
    level = (level * 8.0).astype(F16).reshape(4, 128, 2, 256).transpose(0, 2, 1, 3)
    level = lax.all_to_all(level.reshape(8, 128, 256), ("zh", "zl"), 0, 0, tiled=True)
    grad = jnp.sum(level.astype(F32), 0) * 0.125

    new_moment1 = 0.9 * moment1 + 0.1 * grad
    new_moment2 = 0.999 * moment2 + 0.001 * grad * grad
    update = new_moment1 / first_bias / (jnp.sqrt(new_moment2 / second_bias) + 1e-08)
    new_master = master - 0.01 * (update + 0.1 * master)

    own = new_master.astype(BF16)
    z = [own] + [shift(own, "zh", k) for k in (1, 2, 3)]
    first = jnp.concatenate([z[0], z[1]], 0)
    second = jnp.concatenate([z[2], z[3]], 0)
    first = jnp.concatenate([first] + [shift(first, "x", k) for k in (1, 2, 3)], 0)
    second = jnp.concatenate([second] + [shift(second, "y", k) for k in (1, 2, 3)], 0)
    first = [first] + [shift(first, "y", k) for k in (1, 2, 3)]
    second = [second] + [shift(second, "x", k) for k in (1, 2, 3)]
    new_weights = assemble((first, second), where)
    return (new_master, new_moment1, new_moment2, new_weights)


def solution(mesh):
    fine = Mesh(mesh.devices.reshape(4, 4, 4, 2, 2), ("zh", "y", "x", "zl", "c"))
    dp, tensor = ("zh", "y", "x"), ("zl", "c")
    tokens, state = P(dp + tensor, None), P(dp, tensor)
    return jax.shard_map(
        per_device,
        mesh=fine,
        in_specs=(tokens, tokens, state, state, state),
        out_specs=(state, state, state, P(None, tensor)),
        check_vma=False,
    )
```

```python
import math

import jax
import jax.numpy as jnp
from jax import lax
from jax.experimental import pallas as pl
from jax.experimental.pallas import tpu as pltpu
from jax.sharding import Mesh
from jax.sharding import PartitionSpec as P

first_bias = 1.0 - math.exp(100.0 * math.log(0.9))
second_bias = 1.0 - math.exp(100.0 * math.log(0.999))

F32, F16, BF16 = jnp.float32, jnp.float16, jnp.bfloat16
LANES = 128


def shift(array, axis, by, size=4):
    return lax.ppermute(array, axis, [(i, (i + by) % size) for i in range(size)])


def other_core(array):
    return lax.ppermute(array, "c", [(0, 1), (1, 0)])


def arrange(acts, where):
    tokens, rows = acts.shape[0], 32

    def kernel(where_ref, acts_ref, out_ref):
        x, y = where_ref[0], where_ref[1]
        for colour in range(2):
            for first in range(4):
                for second in range(4):
                    kx, ky = (first, second) if colour == 0 else (second, first)
                    for half in range(2):
                        block = (
                            (2 * colour + half) * 16
                            + lax.rem(y + ky, 4) * 4
                            + lax.rem(x + kx, 4)
                        )
                        columns = pl.ds(pl.multiple_of(block * LANES, LANES), LANES)
                        place = pl.ds((second * 2 + half) * LANES, LANES)
                        out_ref[colour * 4 + first, :, place] = acts_ref[:, columns]

    return pl.pallas_call(
        kernel,
        grid_spec=pltpu.PrefetchScalarGridSpec(
            num_scalar_prefetch=1,
            grid=(tokens // rows,),
            in_specs=[pl.BlockSpec((rows, 8192), lambda i, _: (i, 0))],
            out_specs=pl.BlockSpec((8, rows, 1024), lambda i, _: (0, i, 0)),
        ),
        out_shape=jax.ShapeDtypeStruct((8, tokens, 1024), acts.dtype),
        cost_estimate=pl.CostEstimate(
            flops=0, bytes_accessed=4 * acts.size, transcendentals=0
        ),
    )(where, acts)


def assemble(pieces, where):
    def kernel(where_ref, *refs):
        ins, out_ref, sem = refs[:8], refs[8], refs[9]
        x, y, zh = where_ref[0], where_ref[1], where_ref[2]
        copies = []
        for colour in range(2):
            for first in range(4):
                for second in range(4):
                    kx, ky = (second, first) if colour == 0 else (first, second)
                    for half in range(2):
                        kz = 2 * colour + half
                        block = (
                            lax.rem(zh + 4 - kz, 4) * 16
                            + lax.rem(y + 4 - ky, 4) * 4
                            + lax.rem(x + 4 - kx, 4)
                        )
                        copies.append(
                            pltpu.make_async_copy(
                                ins[colour * 4 + first].at[
                                    pl.ds((second * 2 + half) * LANES, LANES), :
                                ],
                                out_ref.at[
                                    pl.ds(pl.multiple_of(block * LANES, LANES), LANES), :
                                ],
                                sem,
                            )
                        )
        for copy in copies:
            copy.start()
        for copy in copies:
            copy.wait()

    return pl.pallas_call(
        kernel,
        out_shape=jax.ShapeDtypeStruct((8192, 256), BF16),
        in_specs=[pl.BlockSpec(memory_space=pltpu.SMEM)]
        + [pl.BlockSpec(memory_space=pltpu.VMEM)] * 8,
        out_specs=pl.BlockSpec(memory_space=pl.ANY),
        scratch_shapes=[pltpu.SemaphoreType.DMA],
    )(where, *pieces[0], *pieces[1])


def dot(a, b):
    return lax.dot_general(a, b, (((0,), (0,)), ((), ())), preferred_element_type=F32)


def per_device(acts, grad_out, master, moment1, moment2):
    x, y, zh, core = (lax.axis_index(name) for name in ("x", "y", "zh", "c"))
    where = jnp.stack([x, y, zh]).astype(jnp.int32)

    parts = grad_out.reshape(-1, 2, 2, 256)
    mine = jnp.where(core == 0, parts[:, :, 0], parts[:, :, 1]).reshape(-1, 512)
    theirs = jnp.where(core == 0, parts[:, :, 1], parts[:, :, 0]).reshape(-1, 512)
    peer_grad = other_core(theirs)
    chunks = arrange(acts, where)
    order = (2, 6, 1, 5, 3, 7, 0, 4)
    partial = {}
    for i in order:
        peer = other_core(chunks[i])
        partial[i] = dot(chunks[i], mine) + dot(peer, peer_grad)

    def reduce(parts_by_distance, axis, scale):
        total = parts_by_distance[0]
        for by in (2, 1, 3):
            sent = (parts_by_distance[by] * scale).astype(F16)
            total = total + shift(sent, axis, by).astype(F32) * (1.0 / scale)
        return total

    sum_x = reduce([partial[k] for k in range(4)], "x", 128.0)
    sum_y = reduce([partial[4 + k] for k in range(4)], "y", 128.0)
    sum_xy = reduce([sum_x[k * 256 : (k + 1) * 256] for k in range(4)], "y", 32.0)
    sum_yx = reduce([sum_y[k * 256 : (k + 1) * 256] for k in range(4)], "x", 32.0)
    level = jnp.concatenate([sum_xy, sum_yx], 0)
    zl = lax.axis_index("zl")
    near, far = level[:, :256], level[:, 256:]
    kept, sent = jnp.where(zl == 0, near, far), jnp.where(zl == 0, far, near)
    sent = lax.ppermute((sent * 8.0).astype(F16), "zl", [(0, 1), (1, 0)])
    level = kept + sent.astype(F32) * 0.125
    rows = [lax.dynamic_slice_in_dim(level, lax.rem(zh + k, 4) * 128, 128) for k in range(4)]
    grad = reduce(rows, "zh", 4.0)

    new_moment1 = 0.9 * moment1 + 0.1 * grad
    new_moment2 = 0.999 * moment2 + 0.001 * grad * grad
    update = new_moment1 / first_bias / (jnp.sqrt(new_moment2 / second_bias) + 1e-08)
    new_master = master - 0.01 * (update + 0.1 * master)

    own = new_master.astype(BF16)
    z = [own] + [shift(own, "zh", k) for k in (1, 2, 3)]
    first = jnp.concatenate([z[0], z[1]], 0)
    second = jnp.concatenate([z[2], z[3]], 0)
    first = jnp.concatenate([first] + [shift(first, "x", k) for k in (1, 2, 3)], 0)
    second = jnp.concatenate([second] + [shift(second, "y", k) for k in (1, 2, 3)], 0)
    first = [first] + [shift(first, "y", k) for k in (1, 2, 3)]
    second = [second] + [shift(second, "x", k) for k in (1, 2, 3)]
    new_weights = assemble((first, second), where)
    return (new_master, new_moment1, new_moment2, new_weights)


def solution(mesh):
    fine = Mesh(mesh.devices.reshape(4, 4, 4, 2, 2), ("zh", "y", "x", "zl", "c"))
    dp, tensor = ("zh", "y", "x"), ("zl", "c")
    tokens, state = P(dp + tensor, None), P(dp, tensor)
    return jax.shard_map(
        per_device,
        mesh=fine,
        in_specs=(tokens, tokens, state, state, state),
        out_specs=(state, state, state, P(None, tensor)),
        check_vma=False,
    )
```

```python
import math

import jax
import jax.numpy as jnp
from jax import lax
from jax.experimental import pallas as pl
from jax.experimental.pallas import tpu as pltpu
from jax.sharding import Mesh
from jax.sharding import PartitionSpec as P

first_bias = 1.0 - math.exp(100.0 * math.log(0.9))
second_bias = 1.0 - math.exp(100.0 * math.log(0.999))

F32, F16, BF16 = jnp.float32, jnp.float16, jnp.bfloat16
BLOCK = 128

FIRST, SECOND = ("x", "x", "y", "y"), ("y", "y", "x", "x")
PAIRS = ((1, 3), (3, 1), (1, 3), (3, 1))
ORDER = ((0, 3, 1, 2), (0, 1, 3, 2), (0, 3, 1, 2), (0, 1, 3, 2))


def swap(array, axis, by, size=4):
    return lax.ppermute(array, axis, [(i, i ^ by) for i in range(size)])


def owner(part, first, second, x, y):
    x_by, y_by = (first, second) if FIRST[part] == "x" else (second, first)
    return lax.bitwise_xor(y, y_by) * 4 + lax.bitwise_xor(x, x_by)


def arrange(acts, where):
    tokens, rows = acts.shape[0], 32

    def kernel(where_ref, acts_ref, kept_ref, *sent_refs):
        x, y = where_ref[0], where_ref[1]
        for part in range(4):
            for i, first in enumerate(ORDER[part]):
                for j, second in enumerate(ORDER[part]):
                    block = part * 16 + owner(part, first, second, x, y)
                    columns = acts_ref[:, pl.ds(pl.multiple_of(block * BLOCK, BLOCK), BLOCK)]
                    place = (i % 2) * 4 + j
                    if i < 2:
                        place = part * 8 + place
                        kept_ref[:, place * BLOCK : (place + 1) * BLOCK] = columns
                    else:
                        sent_refs[part][:, place * BLOCK : (place + 1) * BLOCK] = columns

    widths = (4096, 1024, 1024, 1024, 1024)
    return pl.pallas_call(
        kernel,
        grid_spec=pltpu.PrefetchScalarGridSpec(
            num_scalar_prefetch=1,
            grid=(tokens // rows,),
            in_specs=[pl.BlockSpec((rows, 8192), lambda i, _: (i, 0))],
            out_specs=[pl.BlockSpec((rows, width), lambda i, _: (i, 0)) for width in widths],
        ),
        out_shape=[jax.ShapeDtypeStruct((tokens, width), acts.dtype) for width in widths],
        cost_estimate=pl.CostEstimate(
            flops=0, bytes_accessed=4 * acts.size, transcendentals=0
        ),
    )(where, acts)


def assemble(pieces, where):
    def kernel(where_ref, *refs):
        ins, out_ref, sem = refs[:8], refs[8], refs[9]
        x, y, zh = where_ref[0], where_ref[1], where_ref[2]
        copies = []
        for part in range(4):
            order = gather_order(part)
            for i, first in enumerate(order):
                for j, second in enumerate(order):
                    block = lax.bitwise_xor(zh, part) * 16 + owner(part, first, second, x, y)
                    place = (i % 2) * 4 + j
                    copies.append(
                        pltpu.make_async_copy(
                            ins[part * 2 + i // 2].at[pl.ds(place * BLOCK, BLOCK), :],
                            out_ref.at[pl.ds(pl.multiple_of(block * BLOCK, BLOCK), BLOCK), :],
                            sem,
                        )
                    )
        for copy in copies:
            copy.start()
        for copy in copies:
            copy.wait()

    return pl.pallas_call(
        kernel,
        out_shape=jax.ShapeDtypeStruct((8192, 256), BF16),
        in_specs=[pl.BlockSpec(memory_space=pltpu.SMEM)]
        + [pl.BlockSpec(memory_space=pltpu.VMEM)] * 8,
        out_specs=pl.BlockSpec(memory_space=pl.ANY),
        scratch_shapes=[pltpu.SemaphoreType.DMA],
    )(where, *[half for piece in pieces for half in piece])


def gather_order(part):
    by, then = PAIRS[part]
    return (0, by, then, by ^ then)


def dot(a, b):
    return lax.dot_general(a, b, (((0,), (0,)), ((), ())), preferred_element_type=F32)


def received(array, swapped, scale):
    return swapped((array * scale).astype(F16)).astype(F32) * (1.0 / scale)


def per_device(acts, grad_out, master, moment1, moment2):
    x, y, zh, zl, core = (lax.axis_index(name) for name in ("x", "y", "zh", "zl", "c"))
    where = jnp.stack([x, y, zh]).astype(jnp.int32)
    parts = range(4)

    def halves(array):
        cut = array.reshape(-1, 2, 2, 256)
        low, high = cut[:, :, 0], cut[:, :, 1]
        mine, theirs = jnp.where(core == 0, low, high), jnp.where(core == 0, high, low)
        return mine.reshape(-1, 512), theirs.reshape(-1, 512)

    far_grad = [swap(grad_out, FIRST[s], PAIRS[s][0]) for s in parts]
    mine, theirs = halves(grad_out)
    peer = swap(theirs, "c", 1, 2)
    kept, *sent = arrange(acts, where)
    far_acts = [swap(sent[s], FIRST[s], PAIRS[s][0]) for s in parts]
    peer_kept = swap(kept, "c", 1, 2)
    far_mine, far_theirs = zip(*[halves(far_grad[s]) for s in parts])
    far_peer = swap(jnp.concatenate(far_theirs, 0), "c", 1, 2)
    tokens = acts.shape[0]

    level = []
    for s in parts:
        far_peer_acts = swap(far_acts[s], "c", 1, 2)
        columns = slice(s * 1024, (s + 1) * 1024)
        level.append(
            dot(kept[:, columns], mine)
            + dot(peer_kept[:, columns], peer)
            + dot(far_acts[s], far_mine[s])
            + dot(far_peer_acts, far_peer[s * tokens : (s + 1) * tokens])
        )

    for axes, pair, scale in ((FIRST, 1, 64.0), (SECOND, 0, 32.0), (SECOND, 1, 16.0)):
        for s in parts:
            half = level[s].shape[0] // 2
            far = received(level[s][half:], lambda v: swap(v, axes[s], PAIRS[s][pair]), scale)
            level[s] = level[s][:half] + far

    z_perms = [[(i, i ^ 1) for i in range(8)], [(i, ((i + 1) ^ 1) - 1 & 7) for i in range(8)]]
    rows = []
    for pair in range(2):
        both = jnp.concatenate(level[2 * pair : 2 * pair + 2], 0)
        low, high = both[:, :256], both[:, 256:]
        own, other = jnp.where(zl == 0, low, high), jnp.where(zl == 0, high, low)
        rows.append(own + received(other, lambda v: lax.ppermute(v, ("zh", "zl"), z_perms[pair]), 8.0))
    level = jnp.concatenate(rows, 0)
    block = [
        lax.dynamic_slice_in_dim(level, lax.bitwise_xor(zh, k) * BLOCK, BLOCK) for k in range(4)
    ]
    grad = block[0]
    for k in (2, 1, 3):
        grad = grad + swap(block[k], "zh", k)

    new_moment1 = 0.9 * moment1 + 0.1 * grad
    new_moment2 = 0.999 * moment2 + 0.001 * grad * grad
    update = new_moment1 / first_bias / (jnp.sqrt(new_moment2 / second_bias) + 1e-08)
    new_master = master - 0.01 * (update + 0.1 * master)

    own = new_master.astype(BF16)
    pieces = [own] + [swap(own, "zh", k) for k in (1, 2, 3)]
    for axes, pair in ((SECOND, 0), (SECOND, 1), (FIRST, 0)):
        for s in parts:
            far = swap(pieces[s], axes[s], PAIRS[s][pair])
            pieces[s] = jnp.concatenate([pieces[s], far], 0)
    pieces = [(pieces[s], swap(pieces[s], FIRST[s], PAIRS[s][1])) for s in parts]
    new_weights = assemble(pieces, where)
    return (new_master, new_moment1, new_moment2, new_weights)


def solution(mesh):
    fine = Mesh(mesh.devices.reshape(4, 4, 4, 2, 2), ("zh", "y", "x", "zl", "c"))
    dp, tensor = ("zh", "y", "x"), ("zl", "c")
    tokens, state = P(dp + tensor, None), P(dp, tensor)
    return jax.shard_map(
        per_device,
        mesh=fine,
        in_specs=(tokens, tokens, state, state, state),
        out_specs=(state, state, state, P(None, tensor)),
        check_vma=False,
    )
```

```python
import math

import jax
import jax.numpy as jnp
from jax import lax
from jax.experimental import pallas as pl
from jax.experimental.pallas import tpu as pltpu
from jax.sharding import Mesh
from jax.sharding import PartitionSpec as P

first_bias = 1.0 - math.exp(100.0 * math.log(0.9))
second_bias = 1.0 - math.exp(100.0 * math.log(0.999))

F32, F16, BF16 = jnp.float32, jnp.float16, jnp.bfloat16
BLOCK = 128
VMEM = pltpu.CompilerParams(vmem_limit_bytes=32 * 2**20)

FIRST, SECOND = ("x", "y"), ("y", "x")
NEAR, NEXT = (1, 3), (3, 1)


def swap(array, axis, by):
    pairs = [(2 * i + c, 2 * (i ^ by[c]) + c) for i in range(4) for c in range(2)]
    return lax.ppermute(array, (axis, "c"), pairs)


def other_core(array):
    return lax.ppermute(array, "c", [(0, 1), (1, 0)])


def order(core):
    return 0, 3 - 2 * core, 1 + 2 * core, 2


def owner(part, first, second, x, y):
    x_by, y_by = (first, second) if part == 0 else (second, first)
    return lax.bitwise_xor(y, y_by) * 4 + lax.bitwise_xor(x, x_by)


def other_rows(acts, where):
    half = acts.shape[1] // 4

    def kernel(where_ref, acts_ref, out_ref):
        for part in range(2):
            start = pl.multiple_of((2 * part + 1 - where_ref[3]) * half, half)
            out_ref[:, part * half : (part + 1) * half] = acts_ref[:, pl.ds(start, half)]

    vmem = pl.BlockSpec(memory_space=pltpu.VMEM)
    return pl.pallas_call(
        kernel,
        out_shape=jax.ShapeDtypeStruct((acts.shape[0], 2 * half), acts.dtype),
        in_specs=[pl.BlockSpec(memory_space=pltpu.SMEM), vmem],
        out_specs=vmem,
        compiler_params=VMEM,
        cost_estimate=pl.CostEstimate(
            flops=0, bytes_accessed=2 * acts.size, transcendentals=0
        ),
    )(where, acts)


def arrange(acts, peer, where, sent):
    tokens = acts.shape[0]

    def kernel(where_ref, acts_ref, peer_ref, *out_refs):
        x, y, core = where_ref[0], where_ref[1], where_ref[3]
        distances = order(core)
        for part in range(2):
            for i in range(2):
                for j in range(4):
                    out_ref, place = out_refs[2 * part + i], slice(j * BLOCK, (j + 1) * BLOCK)
                    block = owner(part, distances[2 * sent + i], distances[j], x, y)
                    own = ((2 * part + core) * 16 + block) * BLOCK
                    out_ref[:tokens, place] = acts_ref[:, pl.ds(pl.multiple_of(own, BLOCK), BLOCK)]
                    other = (part * 16 + block) * BLOCK
                    out_ref[tokens:, place] = peer_ref[:, pl.ds(pl.multiple_of(other, BLOCK), BLOCK)]

    out = jax.ShapeDtypeStruct((2 * tokens, 4 * BLOCK), acts.dtype)
    vmem = pl.BlockSpec(memory_space=pltpu.VMEM)
    outs = pl.pallas_call(
        kernel,
        out_shape=[out] * 4,
        in_specs=[pl.BlockSpec(memory_space=pltpu.SMEM), vmem, vmem],
        out_specs=[vmem] * 4,
        compiler_params=VMEM,
        cost_estimate=pl.CostEstimate(
            flops=0, bytes_accessed=16 * out.size, transcendentals=0
        ),
    )(where, acts, peer)
    return [outs[:2], outs[2:]]


def place(pieces, where, half, into=None):
    def kernel(where_ref, *refs):
        ins, out_ref, sem = refs[:2], refs[-2], refs[-1]
        x, y, zh, core = (where_ref[i] for i in range(4))
        distances = (0, 1 + 2 * core, 3 - 2 * core, 2)
        copies = []
        for part in range(2):
            for i in range(2):
                for j in range(4):
                    for k in range(2):
                        block = lax.bitwise_xor(zh, 2 * part + k) * 16
                        block += owner(part, distances[2 * half + i], distances[j], x, y)
                        copies.append(
                            pltpu.make_async_copy(
                                ins[part].at[pl.ds((i * 8 + j * 2 + k) * BLOCK, BLOCK), :],
                                out_ref.at[pl.ds(pl.multiple_of(block * BLOCK, BLOCK), BLOCK), :],
                                sem,
                            )
                        )
        for copy in copies:
            copy.start()
        for copy in copies:
            copy.wait()

    anywhere = pl.BlockSpec(memory_space=pl.ANY)
    return pl.pallas_call(
        kernel,
        out_shape=jax.ShapeDtypeStruct((8192, 256), BF16),
        in_specs=[pl.BlockSpec(memory_space=pltpu.SMEM)]
        + [pl.BlockSpec(memory_space=pltpu.VMEM)] * 2
        + [anywhere] * (into is not None),
        out_specs=anywhere,
        scratch_shapes=[pltpu.SemaphoreType.DMA],
        input_output_aliases={} if into is None else {3: 0},
        compiler_params=VMEM,
        cost_estimate=pl.CostEstimate(
            flops=0, bytes_accessed=8 * 2**20, transcendentals=0
        ),
    )(where, *pieces, *(() if into is None else (into,)))


def dot(a, b):
    return lax.dot_general(a, b, (((0,), (0,)), ((), ())), preferred_element_type=F32)


def received(array, swapped, scale):
    return swapped((array * scale).astype(F16)).astype(F32) * (1.0 / scale)


def per_device(acts, grad_out, master, moment1, moment2):
    x, y, zh, zl, core = (lax.axis_index(name) for name in ("x", "y", "zh", "zl", "c"))
    where = jnp.stack([x, y, zh, core]).astype(jnp.int32)
    parts = range(2)

    chip_grad = jnp.concatenate([grad_out, other_core(grad_out)], 0)
    peer = other_core(other_rows(acts, where))

    far_grad = [swap(chip_grad, FIRST[p], NEAR) for p in parts]
    sent = arrange(acts, peer, where, 1)
    far_acts = [[None, None], [None, None]]
    for i in (1, 0):
        for p in parts:
            far_acts[p][i] = swap(sent[p][i], FIRST[p], NEAR)
    kept = arrange(acts, peer, where, 0)

    def partial(p, i):
        return dot(kept[p][i], chip_grad) + dot(far_acts[p][i], far_grad[p])

    passed = [partial(p, 1) for p in parts]
    late = [received(passed[p][256:], lambda v: swap(v, FIRST[p], NEXT), 64.0) for p in parts]
    soon = [received(passed[p][:256], lambda v: swap(v, FIRST[p], NEXT), 64.0) for p in parts]
    own = [partial(p, 0) for p in parts]
    level = [
        own[p][:256] + soon[p] + received(own[p][256:] + late[p], lambda v: swap(v, SECOND[p], NEAR), 32.0)
        for p in parts
    ]
    level = [
        level[p][:128] + received(level[p][128:], lambda v: swap(v, SECOND[p], NEXT), 16.0)
        for p in parts
    ]

    both = jnp.concatenate(level, 0)
    low, high = both[:, :512], both[:, 512:]
    pairs = [
        (2 * z + c, 2 * (z ^ 1 if c == 0 else ((z + 1) ^ 1) - 1 & 7) + c)
        for z in range(8)
        for c in range(2)
    ]
    level = jnp.where(zl == 0, low, high) + received(
        jnp.where(zl == 0, high, low), lambda v: lax.ppermute(v, ("zh", "zl", "c"), pairs), 8.0
    )
    grad = 0.0
    for j in (1, 0):
        rows = jnp.where(lax.bitwise_xor(zh // 2, j) == 0, level[:128], level[128:])
        for k in (1, 0):
            block = jnp.where(lax.bitwise_xor(zh % 2, k) == 0, rows[:, :256], rows[:, 256:])
            pairs = [
                (2 * z + c, 2 * (c + 2 * ((z // 2) ^ j)) + ((z % 2) ^ k))
                for z in range(4)
                for c in range(2)
            ]
            grad = grad + lax.ppermute(block, ("zh", "c"), pairs)

    new_moment1 = 0.9 * moment1 + 0.1 * grad
    new_moment2 = 0.999 * moment2 + 0.001 * grad * grad
    update = new_moment1 / first_bias / (jnp.sqrt(new_moment2 / second_bias) + 1e-08)
    new_master = master - 0.01 * (update + 0.1 * master)

    own = new_master.astype(BF16)
    z = [own] + [
        lax.ppermute(own, "zh", [(i, i ^ k) for i in range(4)]) for k in (1, 2, 3)
    ]
    pieces = [jnp.concatenate(z[:2], 0), jnp.concatenate(z[2:], 0)]
    for axes, by in ((SECOND, NEAR), (SECOND, NEXT), (FIRST, NEAR)):
        pieces = [jnp.concatenate([pieces[p], swap(pieces[p], axes[p], by)], 0) for p in parts]
    last = [swap(pieces[p], FIRST[p], NEXT) for p in parts]
    new_weights = place(last, where, 1, place(pieces, where, 0))
    return (new_master, new_moment1, new_moment2, new_weights)


def solution(mesh):
    fine = Mesh(mesh.devices.reshape(4, 4, 4, 2, 2), ("zh", "y", "x", "zl", "c"))
    dp, tensor = ("zh", "y", "x"), ("zl", "c")
    tokens, state = P(dp + tensor, None), P(dp, tensor)
    return jax.shard_map(
        per_device,
        mesh=fine,
        in_specs=(tokens, tokens, state, state, state),
        out_specs=(state, state, state, P(None, tensor)),
        check_vma=False,
    )
```

```python
import math

import jax
import jax.numpy as jnp
from jax import lax
from jax.experimental import pallas as pl
from jax.experimental.pallas import tpu as pltpu
from jax.sharding import Mesh
from jax.sharding import PartitionSpec as P

first_bias = 1.0 - math.exp(100.0 * math.log(0.9))
second_bias = 1.0 - math.exp(100.0 * math.log(0.999))

F32, F16, BF16 = jnp.float32, jnp.float16, jnp.bfloat16
BLOCK = 128
VMEM = pltpu.CompilerParams(vmem_limit_bytes=32 * 2**20)

FIRST, SECOND = ("x", "y"), ("y", "x")
NEAR, NEXT = (1, 3), (3, 1)


def swap(array, axis, by, cross=False):
    pairs = [(2 * i + (c ^ cross), 2 * (i ^ by[c]) + c) for i in range(4) for c in range(2)]
    return lax.ppermute(array, (axis, "c"), pairs)


def other_core(array):
    return lax.ppermute(array, "c", [(0, 1), (1, 0)])


def order(core):
    return 0, 3 - 2 * core, 1 + 2 * core, 2


def owner(part, first, second, x, y):
    x_by, y_by = (first, second) if part == 0 else (second, first)
    return lax.bitwise_xor(y, y_by) * 4 + lax.bitwise_xor(x, x_by)


def other_rows(acts, where):
    half = acts.shape[1] // 4

    def kernel(where_ref, acts_ref, out_ref):
        for part in range(2):
            start = pl.multiple_of((2 * part + 1 - where_ref[3]) * half, half)
            out_ref[:, part * half : (part + 1) * half] = acts_ref[:, pl.ds(start, half)]

    vmem = pl.BlockSpec(memory_space=pltpu.VMEM)
    return pl.pallas_call(
        kernel,
        out_shape=jax.ShapeDtypeStruct((acts.shape[0], 2 * half), acts.dtype),
        in_specs=[pl.BlockSpec(memory_space=pltpu.SMEM), vmem],
        out_specs=vmem,
        compiler_params=VMEM,
        cost_estimate=pl.CostEstimate(
            flops=0, bytes_accessed=2 * acts.size, transcendentals=0
        ),
    )(where, acts)


def arrange(acts, peer, where, index):
    tokens = acts.shape[0]

    def kernel(where_ref, acts_ref, peer_ref, *out_refs):
        x, y, core = where_ref[0], where_ref[1], where_ref[3]
        distances = order(core)
        for part in range(2):
            for j in range(4):
                out_ref, place = out_refs[part], slice(j * BLOCK, (j + 1) * BLOCK)
                block = owner(part, distances[index], distances[j], x, y)
                own = ((2 * part + core) * 16 + block) * BLOCK
                out_ref[:tokens, place] = acts_ref[:, pl.ds(pl.multiple_of(own, BLOCK), BLOCK)]
                other = (part * 16 + block) * BLOCK
                out_ref[tokens:, place] = peer_ref[:, pl.ds(pl.multiple_of(other, BLOCK), BLOCK)]

    out = jax.ShapeDtypeStruct((2 * tokens, 4 * BLOCK), acts.dtype)
    vmem = pl.BlockSpec(memory_space=pltpu.VMEM)
    return pl.pallas_call(
        kernel,
        out_shape=[out] * 2,
        in_specs=[pl.BlockSpec(memory_space=pltpu.SMEM), vmem, vmem],
        out_specs=[vmem] * 2,
        compiler_params=VMEM,
        cost_estimate=pl.CostEstimate(
            flops=0, bytes_accessed=8 * out.size, transcendentals=0
        ),
    )(where, acts, peer)


def place(pieces, where, firsts, into=None):
    many = len(pieces)

    def kernel(where_ref, *refs):
        ins, out_ref, sem = refs[:many], refs[-2], refs[-1]
        x, y, zh, core = (where_ref[i] for i in range(4))
        distances = (0, 1 + 2 * core, 3 - 2 * core, 2)
        copies = []
        for part in range(2):
            for i, first in enumerate(firsts):
                for j in range(4):
                    for k in range(2):
                        block = lax.bitwise_xor(zh, 2 * part + k) * 16
                        block += owner(part, distances[first], distances[j], x, y)
                        copies.append(
                            pltpu.make_async_copy(
                                ins[part * len(firsts) + i].at[pl.ds((j * 2 + k) * BLOCK, BLOCK), :],
                                out_ref.at[pl.ds(pl.multiple_of(block * BLOCK, BLOCK), BLOCK), :],
                                sem,
                            )
                        )
        for copy in copies:
            copy.start()
        for copy in copies:
            copy.wait()

    anywhere = pl.BlockSpec(memory_space=pl.ANY)
    return pl.pallas_call(
        kernel,
        out_shape=jax.ShapeDtypeStruct((8192, 256), BF16),
        in_specs=[pl.BlockSpec(memory_space=pltpu.SMEM)]
        + [pl.BlockSpec(memory_space=pltpu.VMEM)] * many
        + [anywhere] * (into is not None),
        out_specs=anywhere,
        scratch_shapes=[pltpu.SemaphoreType.DMA],
        input_output_aliases={} if into is None else {1 + many: 0},
        compiler_params=VMEM,
        cost_estimate=pl.CostEstimate(
            flops=0, bytes_accessed=many * 2**20, transcendentals=0
        ),
    )(where, *pieces, *(() if into is None else (into,)))


def dot(a, b):
    return lax.dot_general(a, b, (((0,), (0,)), ((), ())), preferred_element_type=F32)


def received(array, swapped, scale):
    return swapped((array * scale).astype(F16)).astype(F32) * (1.0 / scale)


def per_device(acts, grad_out, master, moment1, moment2):
    x, y, zh, zl, core = (lax.axis_index(name) for name in ("x", "y", "zh", "zl", "c"))
    where = jnp.stack([x, y, zh, core]).astype(jnp.int32)
    parts = range(2)

    far_grad = [
        jnp.concatenate([swap(grad_out, FIRST[p], NEAR), swap(grad_out, FIRST[p], NEAR, True)], 0)
        for p in parts
    ]
    peer = other_core(other_rows(acts, where))
    sent = arrange(acts, peer, where, 3)
    far_acts = [[None, swap(sent[p], FIRST[p], NEAR)] for p in parts]
    grad_out, far_grad = lax.optimization_barrier((grad_out, far_grad))
    chip_grad = jnp.concatenate([grad_out, other_core(grad_out)], 0)
    later, chip_grad = lax.optimization_barrier((where, chip_grad))
    sent = arrange(acts, peer, later, 2)
    for p in parts:
        far_acts[p][0] = swap(sent[p], FIRST[p], NEAR)
    kept = [arrange(acts, peer, where, i) for i in range(2)]

    def partial(p, i):
        return dot(kept[i][p], chip_grad) + dot(far_acts[p][i], far_grad[p])

    passed = [partial(p, 1) for p in parts]
    late = [received(passed[p][256:], lambda v: swap(v, FIRST[p], NEXT), 64.0) for p in parts]
    soon = [received(passed[p][:256], lambda v: swap(v, FIRST[p], NEXT), 64.0) for p in parts]
    own = [partial(p, 0) for p in parts]
    level = []
    for p in parts:
        upper, lower = own[p][256:] + late[p], own[p][:256] + soon[p]
        level.append(
            lower[:128]
            + received(upper[128:], lambda v: swap(v, SECOND[p], (2, 2)), 32.0)
            + received(upper[:128], lambda v: swap(v, SECOND[p], NEAR), 32.0)
            + received(lower[128:], lambda v: swap(v, SECOND[p], NEXT), 32.0)
        )

    grad = 0.0
    for j, l, k in ((1, 1, 1), (1, 1, 0), (1, 0, 1), (1, 0, 0), (0, 1, 1), (0, 1, 0), (0, 0, 1), (0, 0, 0)):
        rows = jnp.where(lax.bitwise_xor(zh // 2, j) == 0, level[0], level[1])
        rows = jnp.where(lax.bitwise_xor(zl, l) == 0, rows[:, :512], rows[:, 512:])
        block = jnp.where(lax.bitwise_xor(zh % 2, k) == 0, rows[:, :256], rows[:, 256:])
        pairs = [
            (4 * z + 2 * a + c, 4 * (c + 2 * ((z // 2) ^ j)) + 2 * (a ^ l) + ((z % 2) ^ k))
            for z in range(4)
            for a in range(2)
            for c in range(2)
        ]
        grad = grad + received(block, lambda v: lax.ppermute(v, ("zh", "zl", "c"), pairs), 8.0)

    new_moment1 = 0.9 * moment1 + 0.1 * grad
    new_moment2 = 0.999 * moment2 + 0.001 * grad * grad
    update = new_moment1 / first_bias / (jnp.sqrt(new_moment2 / second_bias) + 1e-08)
    new_master = master - 0.01 * (update + 0.1 * master)

    own = new_master.astype(BF16)
    z = [own] + [
        lax.ppermute(own, "zh", [(i, i ^ k) for i in range(4)]) for k in (1, 2, 3)
    ]
    pieces = [jnp.concatenate(z[:2], 0), jnp.concatenate(z[2:], 0)]
    pieces = [
        jnp.concatenate([pieces[p]] + [swap(pieces[p], SECOND[p], by) for by in (NEAR, NEXT, (2, 2))], 0)
        for p in parts
    ]
    near = [swap(pieces[p], FIRST[p], NEAR) for p in parts]
    following = [swap(pieces[p], FIRST[p], NEXT) for p in parts]
    last = [swap(near[p], FIRST[p], NEXT) for p in parts]
    first = [array for p in parts for array in (pieces[p], near[p], following[p])]
    new_weights = place(last, where, (3,), place(first, where, (0, 1, 2)))
    return (new_master, new_moment1, new_moment2, new_weights)


def solution(mesh):
    fine = Mesh(mesh.devices.reshape(4, 4, 4, 2, 2), ("zh", "y", "x", "zl", "c"))
    dp, tensor = ("zh", "y", "x"), ("zl", "c")
    tokens, state = P(dp + tensor, None), P(dp, tensor)
    return jax.shard_map(
        per_device,
        mesh=fine,
        in_specs=(tokens, tokens, state, state, state),
        out_specs=(state, state, state, P(None, tensor)),
        check_vma=False,
    )
```

```python
import math

import jax
import jax.numpy as jnp
from jax import lax
from jax.experimental import pallas as pl
from jax.experimental.pallas import tpu as pltpu
from jax.sharding import Mesh
from jax.sharding import PartitionSpec as P

first_bias = 1.0 - math.exp(100.0 * math.log(0.9))
second_bias = 1.0 - math.exp(100.0 * math.log(0.999))

F32, F16, BF16 = jnp.float32, jnp.float16, jnp.bfloat16
BLOCK = 128
VMEM = pltpu.CompilerParams(vmem_limit_bytes=32 * 2**20)

FIRST, SECOND = ("x", "y"), ("y", "x")
NEAR, NEXT = (1, 3), (3, 1)
GATHER_NEAR, GATHER_NEXT = NEAR, NEXT


def swap(array, axis, by):
    pairs = [(2 * i + c, 2 * (i ^ by[c]) + c) for i in range(4) for c in range(2)]
    return lax.ppermute(array, (axis, "c"), pairs)


def other_core(array):
    return lax.ppermute(array, "c", [(0, 1), (1, 0)])


def order(core):
    return 0, 3 - 2 * core, 1 + 2 * core, 2


def owner(part, first, second, x, y):
    x_by, y_by = (first, second) if part == 0 else (second, first)
    return lax.bitwise_xor(y, y_by) * 4 + lax.bitwise_xor(x, x_by)


def other_rows(acts, where):
    half = acts.shape[1] // 4

    def kernel(where_ref, acts_ref, out_ref, sem):
        copies = []
        for part in range(2):
            start = pl.multiple_of((2 * part + 1 - where_ref[3]) * half, half)
            copies.append(
                pltpu.make_async_copy(
                    acts_ref.at[:, pl.ds(start, half)],
                    out_ref.at[:, pl.ds(part * half, half)],
                    sem.at[part],
                )
            )
        for copy in copies:
            copy.start()
        for copy in copies:
            copy.wait()

    return pl.pallas_call(
        kernel,
        out_shape=jax.ShapeDtypeStruct((acts.shape[0], 2 * half), acts.dtype),
        in_specs=[
            pl.BlockSpec(memory_space=pltpu.SMEM),
            pl.BlockSpec(memory_space=pltpu.HBM),
        ],
        out_specs=pl.BlockSpec(memory_space=pltpu.VMEM),
        scratch_shapes=[pltpu.SemaphoreType.DMA((2,))],
        compiler_params=pltpu.CompilerParams(vmem_limit_bytes=58 * 2**20),
        cost_estimate=pl.CostEstimate(
            flops=0, bytes_accessed=2 * acts.size, transcendentals=0
        ),
    )(where, acts)


def arrange(acts, peer, where, index):
    tokens = acts.shape[0]

    def kernel(where_ref, acts_ref, peer_ref, *out_refs):
        x, y, core = where_ref[0], where_ref[1], where_ref[3]
        distances = order(core)
        for part in range(2):
            for j in range(4):
                out_ref, place = out_refs[part], slice(j * BLOCK, (j + 1) * BLOCK)
                block = owner(part, distances[index], distances[j], x, y)
                own = ((2 * part + core) * 16 + block) * BLOCK
                out_ref[:tokens, place] = acts_ref[:, pl.ds(pl.multiple_of(own, BLOCK), BLOCK)]
                other = (part * 16 + block) * BLOCK
                out_ref[tokens:, place] = peer_ref[:, pl.ds(pl.multiple_of(other, BLOCK), BLOCK)]

    out = jax.ShapeDtypeStruct((2 * tokens, 4 * BLOCK), acts.dtype)
    vmem = pl.BlockSpec(memory_space=pltpu.VMEM)
    return pl.pallas_call(
        kernel,
        out_shape=[out] * 2,
        in_specs=[pl.BlockSpec(memory_space=pltpu.SMEM), vmem, vmem],
        out_specs=[vmem] * 2,
        compiler_params=VMEM,
        cost_estimate=pl.CostEstimate(
            flops=0, bytes_accessed=8 * out.size, transcendentals=0
        ),
    )(where, acts, peer)


def place(pieces, where, parts, firsts, into=None):
    many = len(pieces)

    def kernel(where_ref, *refs):
        ins, out_ref, sem = refs[:many], refs[-2], refs[-1]
        x, y, zh, core = (where_ref[i] for i in range(4))
        distances = (0, GATHER_NEAR[0] + (GATHER_NEAR[1] - GATHER_NEAR[0]) * core, GATHER_NEXT[0] + (GATHER_NEXT[1] - GATHER_NEXT[0]) * core, 2)
        copies = []
        for index, part in enumerate(parts):
            for i, first in enumerate(firsts):
                for j in range(4):
                    for k in range(2):
                        block = lax.bitwise_xor(zh, distances[2 * part + k]) * 16
                        block += owner(part, distances[first], distances[j], x, y)
                        copies.append(
                            pltpu.make_async_copy(
                                ins[index * len(firsts) + i].at[pl.ds((j * 2 + k) * BLOCK, BLOCK), :],
                                out_ref.at[pl.ds(pl.multiple_of(block * BLOCK, BLOCK), BLOCK), :],
                                sem,
                            )
                        )
        for copy in copies:
            copy.start()
        for copy in copies:
            copy.wait()

    anywhere = pl.BlockSpec(memory_space=pl.ANY)
    return pl.pallas_call(
        kernel,
        out_shape=jax.ShapeDtypeStruct((8192, 256), BF16),
        in_specs=[pl.BlockSpec(memory_space=pltpu.SMEM)]
        + [pl.BlockSpec(memory_space=pltpu.VMEM)] * many
        + [anywhere] * (into is not None),
        out_specs=anywhere,
        scratch_shapes=[pltpu.SemaphoreType.DMA],
        input_output_aliases={} if into is None else {1 + many: 0},
        compiler_params=VMEM,
        cost_estimate=pl.CostEstimate(
            flops=0, bytes_accessed=many * 2**20, transcendentals=0
        ),
    )(where, *pieces, *(() if into is None else (into,)))


def dot(a, b):
    return lax.dot_general(a, b, (((0,), (0,)), ((), ())), preferred_element_type=F32)


def received(array, swapped, scale):
    return swapped((array * scale).astype(F16)).astype(F32) * (1.0 / scale)


def per_device(acts, grad_out, master, moment1, moment2):
    x, y, zh, zl, core = (lax.axis_index(name) for name in ("x", "y", "zh", "zl", "c"))
    where = jnp.stack([x, y, zh, core]).astype(jnp.int32)
    parts = range(2)

    peer_grad = other_core(grad_out)
    soon_where, peer_grad = lax.optimization_barrier((where, peer_grad))
    chip_grad = jnp.concatenate([grad_out, peer_grad], 0)
    peer = other_core(other_rows(acts, soon_where))

    far_grad = [swap(chip_grad, FIRST[p], NEAR) for p in parts]
    sent, rest = arrange(acts, peer, where, 3), arrange(acts, peer, where, 2)
    kept = [arrange(acts, peer, where, i) for i in range(2)]
    far = [swap(sent[p], FIRST[p], NEAR) for p in parts]
    far, far_grad, rest = lax.optimization_barrier((far, far_grad, rest))
    far_acts = [(swap(rest[p], FIRST[p], NEAR), far[p]) for p in parts]

    near_sums = [[dot(kept[i][p], chip_grad) for i in range(2)] for p in parts]
    near_sums = lax.optimization_barrier(near_sums)

    def partial(p, i):
        return near_sums[p][i] + dot(far_acts[p][i], far_grad[p])

    passed = [
        received(partial(p, 1), lambda v: swap(v, FIRST[p], NEXT), 64.0) for p in parts
    ]
    own = [partial(p, 0) for p in parts]
    upper, lower = [array[256:] for array in passed], [array[:256] for array in passed]
    level = []
    for p in parts:
        far = received(own[p][256:] + upper[p], lambda v: swap(v, SECOND[p], NEAR), 32.0)
        level.append(own[p][:256] + lower[p] + far)
    level = [
        level[p][:128] + received(level[p][128:], lambda v: swap(v, SECOND[p], NEXT), 16.0)
        for p in parts
    ]

    both = jnp.concatenate(level, 0)
    low, high = both[:, :512], both[:, 512:]
    stays, goes = jnp.where(zl == 0, low, high), jnp.where(zl == 0, high, low)

    def by_core(array):
        low, high = array[:, :256], array[:, 256:]
        return jnp.where(core == 0, low, high), jnp.where(core == 0, high, low)

    def along_z(cross):
        pairs = [
            (2 * z + c, 2 * (z ^ 1 if c == 0 else ((z + 1) ^ 1) - 1 & 7) + (c ^ cross))
            for z in range(8)
            for c in range(2)
        ]
        return lambda v: lax.ppermute(v, ("zh", "zl", "c"), pairs)

    straight, crossing = by_core(goes)
    mine, theirs = by_core(stays)
    mine = mine + received(straight, along_z(0), 8.0)
    theirs = other_core(theirs) + received(crossing, along_z(1), 8.0)
    even, odd = jnp.where(core == 0, mine, theirs), jnp.where(core == 0, theirs, mine)
    rows = jnp.concatenate([even[:128], odd[:128], even[128:], odd[128:]], 0)
    block = [
        lax.dynamic_slice_in_dim(rows, lax.bitwise_xor(zh, distance) * BLOCK, BLOCK)
        for distance in order(core)
    ]
    far = swap(jnp.concatenate(block[2:], 0), "zh", NEAR)
    grad = swap(block[1] + far[128:], "zh", NEXT) + (block[0] + far[:128])

    new_moment1 = 0.9 * moment1 + 0.1 * grad
    new_moment2 = 0.999 * moment2 + 0.001 * grad * grad
    update = new_moment1 / first_bias / (jnp.sqrt(new_moment2 / second_bias) + 1e-08)
    new_master = master - 0.01 * (update + 0.1 * master)

    own = new_master.astype(BF16)
    every = (GATHER_NEAR, GATHER_NEXT, (2, 2))
    z = [own] + [swap(own, "zh", by) for by in every]
    pieces = [jnp.concatenate(z[:2], 0), jnp.concatenate(z[2:], 0)]
    far = [swap(pieces[0], SECOND[0], by) for by in every]
    pieces[1], far[0] = lax.optimization_barrier((pieces[1], far[0]))
    pieces[0] = jnp.concatenate([pieces[0]] + far, 0)
    pieces[1] = jnp.concatenate([pieces[1]] + [swap(pieces[1], SECOND[1], by) for by in every], 0)
    near = [swap(pieces[p], FIRST[p], GATHER_NEAR) for p in parts]
    following = [swap(pieces[p], FIRST[p], GATHER_NEXT) for p in parts]
    last = [swap(near[p], FIRST[p], GATHER_NEXT) for p in parts]
    first = [array for p in parts for array in (pieces[p], near[p], following[p])]
    new_weights = place(first, where, parts, (0, 1, 2))
    for p in parts:
        new_weights = place([last[p]], where, (p,), (3,), new_weights)
    return (new_master, new_moment1, new_moment2, new_weights)


def solution(mesh):
    fine = Mesh(mesh.devices.reshape(4, 4, 4, 2, 2), ("zh", "y", "x", "zl", "c"))
    dp, tensor = ("zh", "y", "x"), ("zl", "c")
    tokens, state = P(dp + tensor, None), P(dp, tensor)
    return jax.shard_map(
        per_device,
        mesh=fine,
        in_specs=(tokens, tokens, state, state, state),
        out_specs=(state, state, state, P(None, tensor)),
        check_vma=False,
    )
```

```python
import math

import jax
import jax.numpy as jnp
from jax import lax
from jax.experimental import pallas as pl
from jax.experimental.pallas import tpu as pltpu
from jax.sharding import Mesh
from jax.sharding import PartitionSpec as P

first_bias = 1.0 - math.exp(100.0 * math.log(0.9))
second_bias = 1.0 - math.exp(100.0 * math.log(0.999))

F32, F16, BF16 = jnp.float32, jnp.float16, jnp.bfloat16
BLOCK = 128
VMEM = pltpu.CompilerParams(vmem_limit_bytes=32 * 2**20)

FIRST, SECOND = ("x", "y"), ("y", "x")
NEAR, NEXT = (1, 3), (3, 1)
GATHER_NEAR, GATHER_NEXT = NEAR, NEXT


def swap(array, axis, by):
    pairs = [(2 * i + c, 2 * (i ^ by[c]) + c) for i in range(4) for c in range(2)]
    return lax.ppermute(array, (axis, "c"), pairs)


def other_core(array):
    return lax.ppermute(array, "c", [(0, 1), (1, 0)])


def order(core):
    return 0, 3 - 2 * core, 1 + 2 * core, 2


def owner(part, first, second, x, y):
    x_by, y_by = (first, second) if part == 0 else (second, first)
    return lax.bitwise_xor(y, y_by) * 4 + lax.bitwise_xor(x, x_by)


def other_rows(acts, where):
    half = acts.shape[1] // 4

    def kernel(where_ref, acts_ref, out_ref):
        for part in range(2):
            start = pl.multiple_of((2 * part + 1 - where_ref[3]) * half, half)
            out_ref[:, part * half : (part + 1) * half] = acts_ref[:, pl.ds(start, half)]

    vmem = pl.BlockSpec(memory_space=pltpu.VMEM)
    return pl.pallas_call(
        kernel,
        out_shape=jax.ShapeDtypeStruct((acts.shape[0], 2 * half), acts.dtype),
        in_specs=[pl.BlockSpec(memory_space=pltpu.SMEM), vmem],
        out_specs=vmem,
        compiler_params=VMEM,
        cost_estimate=pl.CostEstimate(
            flops=0, bytes_accessed=2 * acts.size, transcendentals=0
        ),
    )(where, acts)


def arrange(acts, peer, where, index):
    tokens = acts.shape[0]

    def kernel(where_ref, acts_ref, peer_ref, *out_refs):
        x, y, core = where_ref[0], where_ref[1], where_ref[3]
        distances = order(core)
        for part in range(2):
            for j in range(4):
                out_ref, place = out_refs[part], slice(j * BLOCK, (j + 1) * BLOCK)
                block = owner(part, distances[index], distances[j], x, y)
                own = ((2 * part + core) * 16 + block) * BLOCK
                out_ref[:tokens, place] = acts_ref[:, pl.ds(pl.multiple_of(own, BLOCK), BLOCK)]
                other = (part * 16 + block) * BLOCK
                out_ref[tokens:, place] = peer_ref[:, pl.ds(pl.multiple_of(other, BLOCK), BLOCK)]

    out = jax.ShapeDtypeStruct((2 * tokens, 4 * BLOCK), acts.dtype)
    vmem = pl.BlockSpec(memory_space=pltpu.VMEM)
    return pl.pallas_call(
        kernel,
        out_shape=[out] * 2,
        in_specs=[pl.BlockSpec(memory_space=pltpu.SMEM), vmem, vmem],
        out_specs=[vmem] * 2,
        compiler_params=VMEM,
        cost_estimate=pl.CostEstimate(
            flops=0, bytes_accessed=8 * out.size, transcendentals=0
        ),
    )(where, acts, peer)


def place(pieces, where, parts, firsts, into=None):
    many = len(pieces)

    def kernel(where_ref, *refs):
        ins, out_ref, sem = refs[:many], refs[-2], refs[-1]
        x, y, zh, core = (where_ref[i] for i in range(4))
        distances = (0, GATHER_NEAR[0] + (GATHER_NEAR[1] - GATHER_NEAR[0]) * core, GATHER_NEXT[0] + (GATHER_NEXT[1] - GATHER_NEXT[0]) * core, 2)
        copies = []
        for index, part in enumerate(parts):
            for i, first in enumerate(firsts):
                for j in range(4):
                    for k in range(2):
                        block = lax.bitwise_xor(zh, distances[2 * part + k]) * 16
                        block += owner(part, distances[first], distances[j], x, y)
                        copies.append(
                            pltpu.make_async_copy(
                                ins[index * len(firsts) + i].at[pl.ds((j * 2 + k) * BLOCK, BLOCK), :],
                                out_ref.at[pl.ds(pl.multiple_of(block * BLOCK, BLOCK), BLOCK), :],
                                sem,
                            )
                        )
        for copy in copies:
            copy.start()
        for copy in copies:
            copy.wait()

    anywhere = pl.BlockSpec(memory_space=pl.ANY)
    return pl.pallas_call(
        kernel,
        out_shape=jax.ShapeDtypeStruct((8192, 256), BF16),
        in_specs=[pl.BlockSpec(memory_space=pltpu.SMEM)]
        + [pl.BlockSpec(memory_space=pltpu.VMEM)] * many
        + [anywhere] * (into is not None),
        out_specs=anywhere,
        scratch_shapes=[pltpu.SemaphoreType.DMA],
        input_output_aliases={} if into is None else {1 + many: 0},
        compiler_params=VMEM,
        cost_estimate=pl.CostEstimate(
            flops=0, bytes_accessed=many * 2**20, transcendentals=0
        ),
    )(where, *pieces, *(() if into is None else (into,)))


def dot(a, b):
    return lax.dot_general(a, b, (((0,), (0,)), ((), ())), preferred_element_type=F32)


def received(array, swapped, scale):
    return swapped((array * scale).astype(F16)).astype(F32) * (1.0 / scale)


def per_device(acts, grad_out, master, moment1, moment2):
    x, y, zh, zl, core = (lax.axis_index(name) for name in ("x", "y", "zh", "zl", "c"))
    where = jnp.stack([x, y, zh, core]).astype(jnp.int32)
    parts = range(2)

    peer, peer_grad = lax.optimization_barrier((other_rows(acts, where), other_core(grad_out)))
    peer = other_core(peer)
    chip_grad = jnp.concatenate([grad_out, peer_grad], 0)

    far_grad = [swap(chip_grad, FIRST[p], NEAR) for p in parts]
    sent, rest = arrange(acts, peer, where, 3), arrange(acts, peer, where, 2)
    kept = [arrange(acts, peer, where, i) for i in range(2)]
    far = [swap(sent[p], FIRST[p], NEAR) for p in parts]
    far, far_grad, rest = lax.optimization_barrier((far, far_grad, rest))
    far_acts = [(swap(rest[p], FIRST[p], NEAR), far[p]) for p in parts]

    near_sums = [[dot(kept[i][p], chip_grad) for i in range(2)] for p in parts]
    near_sums = lax.optimization_barrier(near_sums)

    def partial(p, i):
        return near_sums[p][i] + dot(far_acts[p][i], far_grad[p])

    passed = [
        received(partial(p, 1), lambda v: swap(v, FIRST[p], NEXT), 64.0) for p in parts
    ]
    own = [partial(p, 0) for p in parts]
    upper, lower = [array[256:] for array in passed], [array[:256] for array in passed]
    level = []
    for p in parts:
        far = received(own[p][256:] + upper[p], lambda v: swap(v, SECOND[p], NEAR), 32.0)
        level.append(own[p][:256] + lower[p] + far)
    level = [
        level[p][:128] + received(level[p][128:], lambda v: swap(v, SECOND[p], NEXT), 16.0)
        for p in parts
    ]

    both = jnp.concatenate(level, 0)
    low, high = both[:, :512], both[:, 512:]
    stays, goes = jnp.where(zl == 0, low, high), jnp.where(zl == 0, high, low)

    def by_core(array):
        low, high = array[:, :256], array[:, 256:]
        return jnp.where(core == 0, low, high), jnp.where(core == 0, high, low)

    def along_z(cross):
        pairs = [
            (2 * z + c, 2 * (z ^ 1 if c == 0 else ((z + 1) ^ 1) - 1 & 7) + (c ^ cross))
            for z in range(8)
            for c in range(2)
        ]
        return lambda v: lax.ppermute(v, ("zh", "zl", "c"), pairs)

    straight, crossing = by_core(goes)
    mine, theirs = by_core(stays)
    mine = mine + received(straight, along_z(0), 8.0)
    theirs = other_core(theirs) + received(crossing, along_z(1), 8.0)
    even, odd = jnp.where(core == 0, mine, theirs), jnp.where(core == 0, theirs, mine)
    rows = jnp.concatenate([even[:128], odd[:128], even[128:], odd[128:]], 0)
    block = [
        lax.dynamic_slice_in_dim(rows, lax.bitwise_xor(zh, distance) * BLOCK, BLOCK)
        for distance in order(core)
    ]
    far = swap(jnp.concatenate(block[2:], 0), "zh", NEAR)
    grad = swap(block[1] + far[128:], "zh", NEXT) + (block[0] + far[:128])

    new_moment1 = 0.9 * moment1 + 0.1 * grad
    new_moment2 = 0.999 * moment2 + 0.001 * grad * grad
    update = new_moment1 / first_bias / (jnp.sqrt(new_moment2 / second_bias) + 1e-08)
    new_master = master - 0.01 * (update + 0.1 * master)

    own = new_master.astype(BF16)
    every = (GATHER_NEAR, GATHER_NEXT, (2, 2))
    z = [own] + [swap(own, "zh", by) for by in every]
    pieces = [jnp.concatenate(z[:2], 0), jnp.concatenate(z[2:], 0)]
    far = [swap(pieces[0], SECOND[0], by) for by in every]
    pieces[1], far[0] = lax.optimization_barrier((pieces[1], far[0]))
    pieces[0] = jnp.concatenate([pieces[0]] + far, 0)
    pieces[1] = jnp.concatenate([pieces[1]] + [swap(pieces[1], SECOND[1], by) for by in every], 0)
    near = [swap(pieces[p], FIRST[p], GATHER_NEAR) for p in parts]
    following = [swap(pieces[p], FIRST[p], GATHER_NEXT) for p in parts]
    last = [swap(near[p], FIRST[p], GATHER_NEXT) for p in parts]
    first = [array for p in parts for array in (pieces[p], near[p], following[p])]
    new_weights = place(first, where, parts, (0, 1, 2))
    for p in parts:
        new_weights = place([last[p]], where, (p,), (3,), new_weights)
    return (new_master, new_moment1, new_moment2, new_weights)


def solution(mesh):
    fine = Mesh(mesh.devices.reshape(4, 4, 4, 2, 2), ("zh", "y", "x", "zl", "c"))
    dp, tensor = ("zh", "y", "x"), ("zl", "c")
    tokens, state = P(dp + tensor, None), P(dp, tensor)
    return jax.shard_map(
        per_device,
        mesh=fine,
        in_specs=(tokens, tokens, state, state, state),
        out_specs=(state, state, state, P(None, tensor)),
        check_vma=False,
    )
```

```python
import math

import jax
import jax.numpy as jnp
from jax import lax
from jax.experimental import pallas as pl
from jax.experimental.pallas import tpu as pltpu
from jax.sharding import Mesh
from jax.sharding import PartitionSpec as P

first_bias = 1.0 - math.exp(100.0 * math.log(0.9))
second_bias = 1.0 - math.exp(100.0 * math.log(0.999))

F32, F16, BF16 = jnp.float32, jnp.float16, jnp.bfloat16
BLOCK = 128
VMEM = pltpu.CompilerParams(vmem_limit_bytes=32 * 2**20)

FIRST, SECOND = ("x", "y"), ("y", "x")
NEAR, NEXT = (1, 3), (3, 1)
GATHER_NEAR, GATHER_NEXT = NEAR, NEXT


def swap(array, axis, by):
    pairs = [(2 * i + c, 2 * (i ^ by[c]) + c) for i in range(4) for c in range(2)]
    return lax.ppermute(array, (axis, "c"), pairs)


def other_core(array):
    return lax.ppermute(array, "c", [(0, 1), (1, 0)])


def order(core):
    return 0, 3 - 2 * core, 1 + 2 * core, 2


def owner(part, first, second, x, y):
    x_by, y_by = (first, second) if part == 0 else (second, first)
    return lax.bitwise_xor(y, y_by) * 4 + lax.bitwise_xor(x, x_by)


def other_rows(acts, where):
    half = acts.shape[1] // 4

    def kernel(where_ref, acts_ref, out_ref):
        for part in range(2):
            start = pl.multiple_of((2 * part + 1 - where_ref[3]) * half, half)
            out_ref[:, part * half : (part + 1) * half] = acts_ref[:, pl.ds(start, half)]

    vmem = pl.BlockSpec(memory_space=pltpu.VMEM)
    return pl.pallas_call(
        kernel,
        out_shape=jax.ShapeDtypeStruct((acts.shape[0], 2 * half), acts.dtype),
        in_specs=[pl.BlockSpec(memory_space=pltpu.SMEM), vmem],
        out_specs=vmem,
        compiler_params=VMEM,
        cost_estimate=pl.CostEstimate(
            flops=0, bytes_accessed=2 * acts.size, transcendentals=0
        ),
    )(where, acts)


def arrange(acts, peer, where, index):
    tokens = acts.shape[0]

    def kernel(where_ref, acts_ref, peer_ref, *out_refs):
        x, y, core = where_ref[0], where_ref[1], where_ref[3]
        distances = order(core)
        for part in range(2):
            for j in range(4):
                out_ref, place = out_refs[part], slice(j * BLOCK, (j + 1) * BLOCK)
                block = owner(part, distances[index], distances[j], x, y)
                own = ((2 * part + core) * 16 + block) * BLOCK
                out_ref[:tokens, place] = acts_ref[:, pl.ds(pl.multiple_of(own, BLOCK), BLOCK)]
                other = (part * 16 + block) * BLOCK
                out_ref[tokens:, place] = peer_ref[:, pl.ds(pl.multiple_of(other, BLOCK), BLOCK)]

    out = jax.ShapeDtypeStruct((2 * tokens, 4 * BLOCK), acts.dtype)
    vmem = pl.BlockSpec(memory_space=pltpu.VMEM)
    return pl.pallas_call(
        kernel,
        out_shape=[out] * 2,
        in_specs=[pl.BlockSpec(memory_space=pltpu.SMEM), vmem, vmem],
        out_specs=[vmem] * 2,
        compiler_params=VMEM,
        cost_estimate=pl.CostEstimate(
            flops=0, bytes_accessed=8 * out.size, transcendentals=0
        ),
    )(where, acts, peer)


def place(pieces, where, specs, into=None):
    many = len(pieces)

    def kernel(where_ref, *refs):
        ins, out_ref, sem = refs[:many], refs[-2], refs[-1]
        x, y, zh, core = (where_ref[i] for i in range(4))
        distances = (0, GATHER_NEAR[0] + (GATHER_NEAR[1] - GATHER_NEAR[0]) * core, GATHER_NEXT[0] + (GATHER_NEXT[1] - GATHER_NEXT[0]) * core, 2)
        copies = []
        for index, (part, first, seconds) in enumerate(specs):
            for j, second in enumerate(seconds):
                for k in range(2):
                    block = lax.bitwise_xor(zh, distances[2 * part + k]) * 16
                    block += owner(part, distances[first], distances[second], x, y)
                    copies.append(
                        pltpu.make_async_copy(
                            ins[index].at[pl.ds((j * 2 + k) * BLOCK, BLOCK), :],
                            out_ref.at[pl.ds(pl.multiple_of(block * BLOCK, BLOCK), BLOCK), :],
                            sem,
                        )
                    )
        for copy in copies:
            copy.start()
        for copy in copies:
            copy.wait()

    anywhere = pl.BlockSpec(memory_space=pl.ANY)
    return pl.pallas_call(
        kernel,
        out_shape=jax.ShapeDtypeStruct((8192, 256), BF16),
        in_specs=[pl.BlockSpec(memory_space=pltpu.SMEM)]
        + [pl.BlockSpec(memory_space=pltpu.VMEM)] * many
        + [anywhere] * (into is not None),
        out_specs=anywhere,
        scratch_shapes=[pltpu.SemaphoreType.DMA],
        input_output_aliases={} if into is None else {1 + many: 0},
        compiler_params=VMEM,
        cost_estimate=pl.CostEstimate(
            flops=0, bytes_accessed=many * 2**20, transcendentals=0
        ),
    )(where, *pieces, *(() if into is None else (into,)))


def dot(a, b):
    return lax.dot_general(a, b, (((0,), (0,)), ((), ())), preferred_element_type=F32)


def received(array, swapped, scale):
    return swapped((array * scale).astype(F16)).astype(F32) * (1.0 / scale)


def per_device(acts, grad_out, master, moment1, moment2):
    x, y, zh, zl, core = (lax.axis_index(name) for name in ("x", "y", "zh", "zl", "c"))
    where = jnp.stack([x, y, zh, core]).astype(jnp.int32)
    parts = range(2)

    peer, peer_grad = lax.optimization_barrier((other_rows(acts, where), other_core(grad_out)))
    peer = other_core(peer)
    chip_grad = jnp.concatenate([grad_out, peer_grad], 0)

    far_grad = [swap(chip_grad, FIRST[p], NEAR) for p in parts]
    sent, rest = arrange(acts, peer, where, 3), arrange(acts, peer, where, 2)
    kept = [arrange(acts, peer, where, i) for i in range(2)]
    far = [swap(sent[p], FIRST[p], NEAR) for p in parts]
    far, far_grad, rest = lax.optimization_barrier((far, far_grad, rest))
    far_acts = [(swap(rest[p], FIRST[p], NEAR), far[p]) for p in parts]

    near_sums = [[dot(kept[i][p], chip_grad) for i in range(2)] for p in parts]
    near_sums = lax.optimization_barrier(near_sums)

    def partial(p, i):
        return near_sums[p][i] + dot(far_acts[p][i], far_grad[p])

    passed = [
        received(partial(p, 1), lambda v: swap(v, FIRST[p], NEXT), 64.0) for p in parts
    ]
    own = [partial(p, 0) for p in parts]
    upper, lower = [array[256:] for array in passed], [array[:256] for array in passed]
    level = []
    for p in parts:
        far = received(own[p][256:] + upper[p], lambda v: swap(v, SECOND[p], NEAR), 32.0)
        level.append(own[p][:256] + lower[p] + far)
    level = [
        level[p][:128] + received(level[p][128:], lambda v: swap(v, SECOND[p], NEXT), 16.0)
        for p in parts
    ]

    both = jnp.concatenate(level, 0)
    low, high = both[:, :512], both[:, 512:]
    stays, goes = jnp.where(zl == 0, low, high), jnp.where(zl == 0, high, low)

    def by_core(array):
        low, high = array[:, :256], array[:, 256:]
        return jnp.where(core == 0, low, high), jnp.where(core == 0, high, low)

    def along_z(cross):
        pairs = [
            (2 * z + c, 2 * (z ^ 1 if c == 0 else ((z + 1) ^ 1) - 1 & 7) + (c ^ cross))
            for z in range(8)
            for c in range(2)
        ]
        return lambda v: lax.ppermute(v, ("zh", "zl", "c"), pairs)

    straight, crossing = by_core(goes)
    mine, theirs = by_core(stays)
    mine = mine + received(straight, along_z(0), 8.0)
    theirs = other_core(theirs) + received(crossing, along_z(1), 8.0)
    even, odd = jnp.where(core == 0, mine, theirs), jnp.where(core == 0, theirs, mine)
    rows = jnp.concatenate([even[:128], odd[:128], even[128:], odd[128:]], 0)
    block = [
        lax.dynamic_slice_in_dim(rows, lax.bitwise_xor(zh, distance) * BLOCK, BLOCK)
        for distance in order(core)
    ]
    far = swap(jnp.concatenate(block[2:], 0), "zh", NEAR)
    grad = swap(block[1] + far[128:], "zh", NEXT) + (block[0] + far[:128])

    new_moment1 = 0.9 * moment1 + 0.1 * grad
    new_moment2 = 0.999 * moment2 + 0.001 * grad * grad
    update = new_moment1 / first_bias / (jnp.sqrt(new_moment2 / second_bias) + 1e-08)
    new_master = master - 0.01 * (update + 0.1 * master)

    own = new_master.astype(BF16)
    every = (GATHER_NEAR, GATHER_NEXT, (2, 2))
    z = [own] + [swap(own, "zh", by) for by in every]
    pieces = [jnp.concatenate(z[:2], 0), jnp.concatenate(z[2:], 0)]
    far = [swap(pieces[0], SECOND[0], by) for by in every]
    pieces[1], far[0] = lax.optimization_barrier((pieces[1], far[0]))
    pieces[0] = jnp.concatenate([pieces[0]] + far, 0)
    far = [swap(pieces[1], SECOND[1], by) for by in every]
    pieces[0], far[0] = lax.optimization_barrier((pieces[0], far[0]))
    pieces[1] = jnp.concatenate([pieces[1]] + far, 0)
    near = [swap(pieces[p], FIRST[p], GATHER_NEAR) for p in parts]
    following = [swap(pieces[p], FIRST[p], GATHER_NEXT) for p in parts]
    last = [
        [swap(near[p][:512], FIRST[p], GATHER_NEXT), swap(following[p][512:], FIRST[p], GATHER_NEAR)]
        for p in parts
    ]
    first = [array for p in parts for array in (pieces[p], near[p], following[p])]
    new_weights = place(first, where, [(p, i, range(4)) for p in parts for i in range(3)])
    for p in parts:
        new_weights = place(last[p], where, [(p, 3, (0, 1)), (p, 3, (2, 3))], new_weights)
    return (new_master, new_moment1, new_moment2, new_weights)


def solution(mesh):
    fine = Mesh(mesh.devices.reshape(4, 4, 4, 2, 2), ("zh", "y", "x", "zl", "c"))
    dp, tensor = ("zh", "y", "x"), ("zl", "c")
    tokens, state = P(dp + tensor, None), P(dp, tensor)
    return jax.shard_map(
        per_device,
        mesh=fine,
        in_specs=(tokens, tokens, state, state, state),
        out_specs=(state, state, state, P(None, tensor)),
        check_vma=False,
    )
```

```python
import math

import jax
import jax.numpy as jnp
from jax import lax
from jax.experimental import pallas as pl
from jax.experimental.pallas import tpu as pltpu
from jax.sharding import Mesh
from jax.sharding import PartitionSpec as P

first_bias = 1.0 - math.exp(100.0 * math.log(0.9))
second_bias = 1.0 - math.exp(100.0 * math.log(0.999))

F32, F16, BF16 = jnp.float32, jnp.float16, jnp.bfloat16
BLOCK = 128
VMEM = pltpu.CompilerParams(vmem_limit_bytes=32 * 2**20)

FIRST, SECOND = ("x", "y"), ("y", "x")
NEAR, NEXT = (1, 3), (3, 1)
GATHER_NEAR, GATHER_NEXT = NEAR, NEXT


def swap(array, axis, by):
    pairs = [(2 * i + c, 2 * (i ^ by[c]) + c) for i in range(4) for c in range(2)]
    return lax.ppermute(array, (axis, "c"), pairs)


def other_core(array):
    return lax.ppermute(array, "c", [(0, 1), (1, 0)])


def order(core):
    return 0, 3 - 2 * core, 1 + 2 * core, 2


def owner(part, first, second, x, y):
    x_by, y_by = (first, second) if part == 0 else (second, first)
    return lax.bitwise_xor(y, y_by) * 4 + lax.bitwise_xor(x, x_by)


def other_rows(acts, where):
    half = acts.shape[1] // 4

    def kernel(where_ref, acts_ref, out_ref):
        for part in range(2):
            start = pl.multiple_of((2 * part + 1 - where_ref[3]) * half, half)
            out_ref[:, part * half : (part + 1) * half] = acts_ref[:, pl.ds(start, half)]

    vmem = pl.BlockSpec(memory_space=pltpu.VMEM)
    return pl.pallas_call(
        kernel,
        out_shape=jax.ShapeDtypeStruct((acts.shape[0], 2 * half), acts.dtype),
        in_specs=[pl.BlockSpec(memory_space=pltpu.SMEM), vmem],
        out_specs=vmem,
        compiler_params=VMEM,
        cost_estimate=pl.CostEstimate(
            flops=0, bytes_accessed=2 * acts.size, transcendentals=0
        ),
    )(where, acts)


def arrange(acts, peer, where, index):
    tokens = acts.shape[0]

    def kernel(where_ref, acts_ref, peer_ref, *out_refs):
        x, y, core = where_ref[0], where_ref[1], where_ref[3]
        distances = order(core)
        for part in range(2):
            for j in range(4):
                out_ref, place = out_refs[part], slice(j * BLOCK, (j + 1) * BLOCK)
                block = owner(part, distances[index], distances[j], x, y)
                own = ((2 * part + core) * 16 + block) * BLOCK
                out_ref[:tokens, place] = acts_ref[:, pl.ds(pl.multiple_of(own, BLOCK), BLOCK)]
                other = (part * 16 + block) * BLOCK
                out_ref[tokens:, place] = peer_ref[:, pl.ds(pl.multiple_of(other, BLOCK), BLOCK)]

    out = jax.ShapeDtypeStruct((2 * tokens, 4 * BLOCK), acts.dtype)
    vmem = pl.BlockSpec(memory_space=pltpu.VMEM)
    return pl.pallas_call(
        kernel,
        out_shape=[out] * 2,
        in_specs=[pl.BlockSpec(memory_space=pltpu.SMEM), vmem, vmem],
        out_specs=[vmem] * 2,
        compiler_params=VMEM,
        cost_estimate=pl.CostEstimate(
            flops=0, bytes_accessed=8 * out.size, transcendentals=0
        ),
    )(where, acts, peer)


def place(pieces, where, specs, into=None):
    many = len(pieces)

    def kernel(where_ref, *refs):
        ins, out_ref, sem = refs[:many], refs[-2], refs[-1]
        x, y, zh, core = (where_ref[i] for i in range(4))
        distances = (0, GATHER_NEAR[0] + (GATHER_NEAR[1] - GATHER_NEAR[0]) * core, GATHER_NEXT[0] + (GATHER_NEXT[1] - GATHER_NEXT[0]) * core, 2)
        copies = []
        for index, (part, first, seconds) in enumerate(specs):
            for j, second in enumerate(seconds):
                for k in range(2):
                    block = lax.bitwise_xor(zh, distances[2 * part + k]) * 16
                    block += owner(part, distances[first], distances[second], x, y)
                    copies.append(
                        pltpu.make_async_copy(
                            ins[index].at[pl.ds((j * 2 + k) * BLOCK, BLOCK), :],
                            out_ref.at[pl.ds(pl.multiple_of(block * BLOCK, BLOCK), BLOCK), :],
                            sem,
                        )
                    )
        for copy in copies:
            copy.start()
        for copy in copies:
            copy.wait()

    anywhere = pl.BlockSpec(memory_space=pl.ANY)
    return pl.pallas_call(
        kernel,
        out_shape=jax.ShapeDtypeStruct((8192, 256), BF16),
        in_specs=[pl.BlockSpec(memory_space=pltpu.SMEM)]
        + [pl.BlockSpec(memory_space=pltpu.VMEM)] * many
        + [anywhere] * (into is not None),
        out_specs=anywhere,
        scratch_shapes=[pltpu.SemaphoreType.DMA],
        input_output_aliases={} if into is None else {1 + many: 0},
        compiler_params=VMEM,
        cost_estimate=pl.CostEstimate(
            flops=0, bytes_accessed=many * 2**20, transcendentals=0
        ),
    )(where, *pieces, *(() if into is None else (into,)))


def dot(a, b):
    return lax.dot_general(a, b, (((0,), (0,)), ((), ())), preferred_element_type=F32)


def received(array, swapped, scale):
    return swapped((array * scale).astype(F16)).astype(F32) * (1.0 / scale)


def per_device(acts, grad_out, master, moment1, moment2):
    x, y, zh, zl, core = (lax.axis_index(name) for name in ("x", "y", "zh", "zl", "c"))
    where = jnp.stack([x, y, zh, core]).astype(jnp.int32)
    parts = range(2)

    peer, peer_grad = lax.optimization_barrier((other_rows(acts, where), other_core(grad_out)))
    peer = other_core(peer)
    chip_grad = jnp.concatenate([grad_out, peer_grad], 0)

    far_grad = [swap(chip_grad, FIRST[p], NEAR) for p in parts]
    sent, rest = arrange(acts, peer, where, 3), arrange(acts, peer, where, 2)
    kept = [arrange(acts, peer, where, i) for i in range(2)]
    far = [swap(sent[p], FIRST[p], NEAR) for p in parts]
    far_grad, rest = lax.optimization_barrier((far_grad, rest))
    far_acts = [(swap(rest[p], FIRST[p], NEAR), far[p]) for p in parts]

    near_sums = [[dot(kept[i][p], chip_grad) for i in range(2)] for p in parts]
    near_sums = lax.optimization_barrier(near_sums)

    def partial(p, i):
        return near_sums[p][i] + dot(far_acts[p][i], far_grad[p])

    passed = [
        received(partial(p, 1), lambda v: swap(v, FIRST[p], NEXT), 64.0) for p in parts
    ]
    own = [partial(p, 0) for p in parts]
    upper, lower = [array[256:] for array in passed], [array[:256] for array in passed]
    level = []
    for p in parts:
        far = received(own[p][256:] + upper[p], lambda v: swap(v, SECOND[p], NEAR), 32.0)
        level.append(own[p][:256] + lower[p] + far)
    level = [
        level[p][:128] + received(level[p][128:], lambda v: swap(v, SECOND[p], NEXT), 16.0)
        for p in parts
    ]

    both = jnp.concatenate(level, 0)
    low, high = both[:, :512], both[:, 512:]
    stays, goes = jnp.where(zl == 0, low, high), jnp.where(zl == 0, high, low)

    def by_core(array):
        low, high = array[:, :256], array[:, 256:]
        return jnp.where(core == 0, low, high), jnp.where(core == 0, high, low)

    def along_z(cross):
        pairs = [
            (2 * z + c, 2 * (z ^ 1 if c == 0 else ((z + 1) ^ 1) - 1 & 7) + (c ^ cross))
            for z in range(8)
            for c in range(2)
        ]
        return lambda v: lax.ppermute(v, ("zh", "zl", "c"), pairs)

    straight, crossing = by_core(goes)
    mine, theirs = by_core(stays)
    mine = mine + received(straight, along_z(0), 8.0)
    theirs = other_core(theirs) + received(crossing, along_z(1), 8.0)
    even, odd = jnp.where(core == 0, mine, theirs), jnp.where(core == 0, theirs, mine)
    rows = jnp.concatenate([even[:128], odd[:128], even[128:], odd[128:]], 0)
    block = [
        lax.dynamic_slice_in_dim(rows, lax.bitwise_xor(zh, distance) * BLOCK, BLOCK)
        for distance in order(core)
    ]
    far = swap(jnp.concatenate(block[2:], 0), "zh", NEAR)
    grad = swap(block[1] + far[128:], "zh", NEXT) + (block[0] + far[:128])

    new_moment1 = 0.9 * moment1 + 0.1 * grad
    new_moment2 = 0.999 * moment2 + 0.001 * grad * grad
    update = new_moment1 / first_bias / (jnp.sqrt(new_moment2 / second_bias) + 1e-08)
    new_master = master - 0.01 * (update + 0.1 * master)

    own = new_master.astype(BF16)
    every = (GATHER_NEAR, GATHER_NEXT, (2, 2))
    z = [own] + [swap(own, "zh", by) for by in every]
    pieces = [jnp.concatenate(z[:2], 0), jnp.concatenate(z[2:], 0)]
    far = [swap(pieces[0], SECOND[0], by) for by in every]
    pieces[0] = jnp.concatenate([pieces[0]] + far, 0)
    far = [swap(pieces[1], SECOND[1], by) for by in every]
    pieces[0], far[2] = lax.optimization_barrier((pieces[0], far[2]))
    pieces[1] = jnp.concatenate([pieces[1]] + far, 0)
    near = [swap(pieces[p], FIRST[p], GATHER_NEAR) for p in parts]
    following = [swap(pieces[p], FIRST[p], GATHER_NEXT) for p in parts]
    last = [
        [swap(near[p][:512], FIRST[p], GATHER_NEXT), swap(following[p][512:], FIRST[p], GATHER_NEAR)]
        for p in parts
    ]
    first = [array for p in parts for array in (pieces[p], near[p], following[p])]
    new_weights = place(first, where, [(p, i, range(4)) for p in parts for i in range(3)])
    for p in parts:
        new_weights = place(last[p], where, [(p, 3, (0, 1)), (p, 3, (2, 3))], new_weights)
    return (new_master, new_moment1, new_moment2, new_weights)


def solution(mesh):
    fine = Mesh(mesh.devices.reshape(4, 4, 4, 2, 2), ("zh", "y", "x", "zl", "c"))
    dp, tensor = ("zh", "y", "x"), ("zl", "c")
    tokens, state = P(dp + tensor, None), P(dp, tensor)
    return jax.shard_map(
        per_device,
        mesh=fine,
        in_specs=(tokens, tokens, state, state, state),
        out_specs=(state, state, state, P(None, tensor)),
        check_vma=False,
    )
```
